32 devices in a mesh: row: 8 (over y, x, core), col: 4 (over z).
Axes of the slice: x: 2, y: 2, z: 4, core: 2. Of those that a mesh axis runs over, the one named last changes fastest.
Arguments:
- collocation: bfloat16 [32768, 2048], P('col', 'row'), may hold values from -6 to 6
- greens: bfloat16 [2, 256, 2048], P(None, None, 'row'), may hold values from -0.0078125 to 0.0078125
- trial_orbitals: bfloat16 [256, 2048], P(None, 'row'), may hold values from -0.125 to 0.125
- coulomb: bfloat16 [4, 8192, 32768], P(None, 'row', 'col'), may hold values from -0.03125 to 0.03125
Outputs:
- gradient: bfloat16 [256, 2, 2048], P('col', None, 'row')
The draws below stay inside these ranges and needn't reach their ends.
All inputs are finite; a program needn't handle non-finite values.
Results may differ from the reference program's by a relative error of at most 0.039.
Values may be sent and summed in bfloat16 or wider, within the bound.
A program may use at most 192 MiB of HBM per device.

```python
import jax
import jax.numpy as jnp
from jax import lax

P_SIZE = 32768
M = 2048
NOCC = 256
WALKERS = 2
N_ROW = 8
N_COL = 4


def shard_levels(rng, extent, pieces, least, high):
    def one(position, blocks):
        steps = jax.random.uniform(jax.random.fold_in(jax.random.fold_in(rng, 6), position), (blocks,), jnp.float32, least / len(pieces), high / len(pieces))
        return jnp.repeat(jnp.exp(steps), extent[position] // blocks).reshape((-1,) + (1,) * (len(extent) - position - 1))

    gain = one(*pieces[0])
    for cut in pieces[1:]:
        gain = gain * one(*cut)
    return gain


def noise(own_key, extent, spread, reach, split=(), kind=jnp.bfloat16):
    factor_of = shard_levels(own_key, extent, split, -0.22, 0.18) if split else 1.0
    entries = jax.random.normal(own_key, extent, jnp.float32) * spread * factor_of
    return jnp.minimum(jnp.maximum(entries, -reach), reach).astype(kind)


def setup_inputs(seed: int = 0) -> dict:
    splits = jax.random.split(jax.random.key(seed), 5)
    return {
        "collocation": noise(splits[0], (P_SIZE, M), 1.0, 6.0, ((0, 4), (1, 8))),
        "greens": noise(splits[1], (WALKERS, NOCC, M), (M * NOCC) ** -0.5, 0.0078125, ((2, 8),)),
        "trial_orbitals": noise(splits[2], (NOCC, M), M ** -0.5, 0.125, ((1, 8),)),
        "coulomb": noise(splits[3], (N_COL, P_SIZE // N_COL, P_SIZE), P_SIZE ** -0.5, 0.03125, ((1, 8), (2, 4))),
    }


def reference(collocation, greens, trial_orbitals, coulomb):
    stacked = jnp.concatenate([trial_orbitals[None], greens], axis=0).reshape((WALKERS + 1) * NOCC, M)
    shard_width = M // N_ROW
    encoded_sum = jnp.zeros((P_SIZE, (WALKERS + 1) * NOCC), jnp.float32)
    for group in range(N_ROW):
        left = collocation[:, group * shard_width:(group + 1) * shard_width].astype(jnp.float32)
        right = stacked[:, group * shard_width:(group + 1) * shard_width].astype(jnp.float32)
        partial_value = jnp.dot(left, right.T, precision=lax.Precision.HIGHEST)
        rounded = lax.optimization_barrier(partial_value.astype(jnp.bfloat16))
        encoded_sum = encoded_sum + rounded.astype(jnp.float32)
    encoded = encoded_sum.astype(jnp.bfloat16)
    orbit = encoded[:, :NOCC]
    orbit_wide = orbit.astype(jnp.float32)
    kernel = coulomb.reshape(P_SIZE, P_SIZE)
    height = min(1024, P_SIZE)
    kernel_blocks = kernel.reshape(P_SIZE // height, height, P_SIZE)
    orbit_blocks = orbit.reshape(P_SIZE // height, height, NOCC)
    results = []
    for walker in range(WALKERS):
        theta = encoded[:, (walker + 1) * NOCC:(walker + 2) * NOCC]
        theta_blocks = theta.reshape(P_SIZE // height, height, NOCC)

        def advance(totals, inputs):
            exchange_sum, potential = totals
            x_block, theta_block, v_block = inputs
            x_wide = x_block.astype(jnp.float32)
            theta_wide = theta_block.astype(jnp.float32)
            v_wide = v_block.astype(jnp.float32)
            t_tile = jnp.dot(theta_wide, orbit_wide.T, precision=lax.Precision.HIGHEST)
            amplitude = (v_wide * t_tile).astype(jnp.bfloat16).astype(jnp.float32)
            exchange_sum = exchange_sum + jnp.dot(amplitude.T, x_wide, precision=lax.Precision.HIGHEST)
            density = jnp.sum(x_wide * theta_wide, axis=1).astype(jnp.bfloat16).astype(jnp.float32)
            potential = potential + jnp.dot(density, v_wide, precision=lax.Precision.HIGHEST)
            return (exchange_sum, potential), None

        start_totals = (jnp.zeros((P_SIZE, NOCC), jnp.float32), jnp.zeros((P_SIZE,), jnp.float32))
        (exchange_sum, potential), unused = lax.scan(advance, start_totals, (orbit_blocks, theta_blocks, kernel_blocks))
        force_walker = (potential[:, None] * orbit_wide - exchange_sum).astype(jnp.bfloat16)
        decoded = jnp.dot(force_walker.astype(jnp.float32).T, collocation.astype(jnp.float32), precision=lax.Precision.HIGHEST)
        results.append(decoded * (P_SIZE ** -0.5))
    return jnp.stack(results, axis=1).astype(jnp.bfloat16)
```

```python
import functools
import math

import jax
import jax.numpy as jnp
from jax import lax
from jax.experimental import pallas as pl
from jax.experimental.pallas import tpu as pltpu
from jax.sharding import PartitionSpec as P

P_SIZE = 32768
NT = (((1,), (1,)), ((), ()))


def force_kernel(walkers, occupied, sub, th_ref, xt_ref, d_ref, xq_ref, xqt_ref, v_ref, o_ref, acc, uacc):
    step, steps = pl.program_id(1), pl.num_programs(1)

    @pl.when(step == 0)
    def _():
        acc[...] = jnp.zeros_like(acc)
        uacc[...] = jnp.zeros_like(uacc)

    for j in range(v_ref.shape[2] // sub):
        qs = slice(j * sub, (j + 1) * sub)
        v = v_ref[0, :, qs]
        for w in range(walkers):
            rows = slice(w * occupied, (w + 1) * occupied)
            tile = lax.dot_general(th_ref[w], xq_ref[qs, :], NT, preferred_element_type=jnp.float32)
            amplitude = tile.astype(jnp.bfloat16) * v
            acc[rows, qs] += jnp.dot(xt_ref[...], amplitude, preferred_element_type=jnp.float32)
        uacc[:, qs] += jnp.dot(d_ref[...], v, preferred_element_type=jnp.float32)

    @pl.when(step == steps - 1)
    def _():
        for w in range(walkers):
            rows = slice(w * occupied, (w + 1) * occupied)
            o_ref[rows, :] = (
                uacc[w : w + 1] * xqt_ref[...].astype(jnp.float32) - acc[rows, :]
            ).astype(jnp.bfloat16)


def partial_forces(theta, x_rows_t, density, x_cols, x_cols_t, coulomb):
    a, b, q = coulomb.shape
    walkers, _, n = theta.shape
    tp, tq = math.gcd(b, 1024), math.gcd(q, 1024)
    sub = math.gcd(tq, 512)
    bp = b // tp
    return pl.pallas_call(
        functools.partial(force_kernel, walkers, n, sub),
        grid=(q // tq, a * bp),
        in_specs=[
            pl.BlockSpec((walkers, tp, n), lambda j, p: (0, p, 0)),
            pl.BlockSpec((n, tp), lambda j, p: (0, p)),
            pl.BlockSpec((density.shape[0], tp), lambda j, p: (0, p)),
            pl.BlockSpec((tq, n), lambda j, p: (j, 0)),
            pl.BlockSpec((n, tq), lambda j, p: (0, j)),
            pl.BlockSpec((1, tp, tq), lambda j, p: (p // bp, p % bp, j)),
        ],
        out_specs=pl.BlockSpec((walkers * n, tq), lambda j, p: (0, j)),
        out_shape=jax.ShapeDtypeStruct((walkers * n, q), jnp.bfloat16),
        scratch_shapes=[
            pltpu.VMEM((walkers * n, tq), jnp.float32),
            pltpu.VMEM((density.shape[0], tq), jnp.float32),
        ],
        compiler_params=pltpu.CompilerParams(vmem_limit_bytes=48 << 20),
    )(theta, x_rows_t, density, x_cols, x_cols_t, coulomb)


def on_device(collocation, greens, trial_orbitals, coulomb):
    walkers, occupied, basis_local = greens.shape
    stacked = jnp.concatenate([trial_orbitals[None], greens], axis=0).reshape(
        (walkers + 1) * occupied, basis_local
    )
    own_collocation = lax.all_to_all(collocation, "row", split_axis=0, concat_axis=1, tiled=True)
    all_stacked = lax.all_gather(stacked, "row", axis=1, tiled=True)
    own_points = lax.dot_general(
        own_collocation, all_stacked, NT, preferred_element_type=jnp.float32
    ).astype(jnp.bfloat16)
    x_cols = lax.all_gather(own_points[:, :occupied], "row", axis=0, tiled=True)
    shard_rows = lax.all_gather(own_points, "col", axis=0, tiled=True)
    x_rows = shard_rows[:, :occupied]
    theta = jnp.stack(
        [shard_rows[:, (w + 1) * occupied : (w + 2) * occupied] for w in range(walkers)]
    )
    density = jnp.sum(
        x_rows.astype(jnp.float32)[None] * theta.astype(jnp.float32), axis=2
    ).astype(jnp.bfloat16)
    density = jnp.pad(density, ((0, -walkers % 16), (0, 0)))
    forces = partial_forces(theta, x_rows.T, density, x_cols, x_cols.T, coulomb)
    forces = lax.psum(forces, "row")
    terms = jnp.dot(forces, collocation, preferred_element_type=jnp.float32)
    terms = terms.astype(jnp.bfloat16).reshape(walkers, occupied, basis_local).transpose(1, 0, 2)
    gradient = lax.psum_scatter(terms, "col", scatter_dimension=0, tiled=True).astype(jnp.float32)
    return (gradient * P_SIZE ** (-0.5)).astype(jnp.bfloat16)


def solution(mesh):
    return jax.shard_map(
        on_device,
        mesh=mesh,
        in_specs=(P("col", "row"), P(None, None, "row"), P(None, "row"), P(None, "row", "col")),
        out_specs=P("col", None, "row"),
        check_vma=False,
    )
```
